32 devices in a mesh: ens: 2 (over y), space: 4 (over z), chan: 2 (over x), sub: 2 (over core).
Axes of the slice: x: 2, y: 2, z: 4, core: 2. Of those that a mesh axis runs over, the one named last changes fastest.
Arguments:
- state_tiles: bfloat16 [128, 16, 128, 128], P(('ens', 'space'), None, ('chan', 'sub')), parts along dimension 0, may hold values from -6 to 6
- water_mask: int32 [64], replicated, may hold values from 0 to 1, as said below
- owner_tiles: int32 [4, 8], replicated, may hold values from 0 to 63, as said below
- neighbors: int32 [64, 3], replicated, may hold values from 0 to 64, as said below
- first_kernel: bfloat16 [3, 3, 16, 256], replicated, may hold values from -0.5 to 0.5
- second_kernel: bfloat16 [3, 3, 256, 512], replicated, may hold values from -0.125 to 0.125
- mix_kernel: bfloat16 [512, 512], P(None, ('chan', 'sub')), may hold values from -0.25 to 0.25
Outputs:
- mixed_out: bfloat16 [64, 32, 32, 512], P(('ens', 'space'), ('chan', 'sub')), parts along dimension 0
The draws below stay inside these ranges and needn't reach their ends.
There are 2 independent parts, one for each index of `ens`. The reference program is written for one: setup_inputs(seed, part) draws one part's arguments, and reference() takes and returns one part's arrays. A program takes and returns all parts, laid end to end along the dimension named above; an argument that names none is the same for every part. Nothing has to cross between parts.
Inputs may be any that keep to these rules, and one draw needn't show every extreme that they name: `water_mask`: exactly 30 tiles are water; all 16 tiles held by one index of space are water. `owner_tiles`: every water tile stands in exactly one slot; the other slots hold a land tile. Each owner holds 7 or 8 water tiles, half of the owners exactly 8. Tile t is held on entry by index t // 16 of space; no owner receives more than 4 water tiles from one such index, and some owner receives exactly 4. `neighbors`: tiles lie on a rectangular grid; 64 stands where a tile lies on the grid's edge and has no such neighbor.
All inputs are finite; a program needn't handle non-finite values.
Results may differ from the reference program's by a relative error of at most 0.0058.
Values may be sent and summed in bfloat16 or wider, within the bound.
A program may use at most 128 MiB of HBM per device.

```python
import jax
import jax.numpy as jnp
from jax import lax

C_IN = 16
C1 = 256
C2 = 512
TS = 128
TPD = 16
CAP = 8
MEMBER_TILES = 64
SLOTS = 32
WATER = 30
N_SPACE = 4


def coast_layout(key):
    keeper_random_key, rank_random_key, pick_key, offset_key, owner_key = jax.random.split(key, 5)
    tile_ids = jnp.arange(MEMBER_TILES, dtype=jnp.int32)
    tile_keeper = tile_ids // TPD
    picked_choice = jax.random.randint(pick_key, (), 0, N_SPACE)
    extra_reward = jax.random.randint(keeper_random_key, (N_SPACE,), 0, 4)
    rank_value = jax.random.randint(rank_random_key, (MEMBER_TILES,), 0, 4096) + extra_reward[tile_keeper] * 1024 + jnp.where(tile_keeper == picked_choice, 100000, 0)
    rank_value = rank_value * MEMBER_TILES + tile_ids
    top_values, water_ids = lax.top_k(rank_value, WATER)
    water_mask = jnp.zeros((MEMBER_TILES,), jnp.int32).at[water_ids].set(1)
    sort_order = jnp.argsort((1 - water_mask) * MEMBER_TILES + tile_ids).astype(jnp.int32)
    water_sorted = sort_order[:WATER]
    land_first = sort_order[WATER]
    offset = jax.random.randint(offset_key, (), 0, N_SPACE // 2 + 1)
    owner_perm = jax.random.permutation(owner_key, N_SPACE).astype(jnp.int32)
    placing = jnp.arange(WATER, dtype=jnp.int32) + offset
    flat_index = owner_perm[placing % N_SPACE] * CAP + placing // N_SPACE
    listing = jnp.full((N_SPACE * CAP,), land_first, jnp.int32).at[flat_index].set(water_sorted)
    return (water_mask, listing.reshape(N_SPACE, CAP))


def draw_water_mask(key, part):
    water_mask, listing = coast_layout(key)
    return water_mask


def draw_owner_tiles(key, part):
    water_mask, listing = coast_layout(key)
    return listing


def draw_neighbors(key, part):
    key = jax.random.fold_in(key, 3)
    position = jax.random.permutation(key, MEMBER_TILES).astype(jnp.int32)
    tile_at = jnp.argsort(position).astype(jnp.int32)
    row_of = position // 16
    col_of = position % 16
    upper = jnp.where(row_of > 0, tile_at[jnp.maximum(position - 16, 0)], MEMBER_TILES)
    left_tile = jnp.where(col_of > 0, tile_at[jnp.maximum(position - 1, 0)], MEMBER_TILES)
    corner = jnp.where((row_of > 0) & (col_of > 0), tile_at[jnp.maximum(position - 17, 0)], MEMBER_TILES)
    return jnp.stack([upper, left_tile, corner], axis=1).astype(jnp.int32)


def block_scale(key, dims, pieces, least, top_value):
    gain = 1.0
    for axis_at, shards_of in pieces:
        heights = jax.random.uniform(jax.random.fold_in(jax.random.fold_in(key, 6), axis_at), (shards_of,), jnp.float32, least / len(pieces), top_value / len(pieces))
        gain = gain * jnp.repeat(jnp.exp(heights), dims[axis_at] // shards_of).reshape((-1,) + (1,) * (len(dims) - 1 - axis_at))
    return gain


def normal_values(own_key, shape, deviation, bound, cuts=(), kind=jnp.bfloat16):
    drawn = jax.random.normal(own_key, shape, jnp.float32) * deviation
    if len(cuts) > 0:
        drawn = block_scale(own_key, shape, cuts, -0.22, 0.18) * drawn
    return jnp.clip(drawn, min=-bound, max=bound).astype(kind)


def setup_inputs(seed: int = 0, part: int = 0) -> dict:
    streams_of = jax.random.split(jax.random.key(seed), 8)
    part_keys = jax.random.split(jax.random.fold_in(streams_of[7], part), 8)
    return {
        "state_tiles": normal_values(part_keys[0], (MEMBER_TILES, C_IN, TS, TS), 1.0, 6.0, ((0, 4), (2, 4))),
        "water_mask": draw_water_mask(jax.random.fold_in(streams_of[7], 71), part),
        "owner_tiles": draw_owner_tiles(jax.random.fold_in(streams_of[7], 71), part),
        "neighbors": draw_neighbors(jax.random.fold_in(streams_of[7], 71), part),
        "first_kernel": normal_values(streams_of[4], (3, 3, C_IN, C1), (9 * C_IN) ** -0.5, 0.5),
        "second_kernel": normal_values(streams_of[5], (3, 3, C1, C2), (9 * C1) ** -0.5, 0.125),
        "mix_kernel": normal_values(streams_of[6], (C2, C2), C2 ** -0.5, 0.25, ((1, 4),)),
    }


def slot_tables(water_mask, owner_tiles, neighbors):
    slot_tile = owner_tiles.reshape(-1)
    tile_ids = jnp.arange(MEMBER_TILES, dtype=jnp.int32)
    live_slots = jnp.sum(jnp.where(slot_tile[:, None] == tile_ids[None, :], water_mask[None, :], 0), axis=1).astype(jnp.int32)
    match_table = (slot_tile[None, :] == tile_ids[:, None]) & (live_slots[None, :] > 0)
    found_any = jnp.any(match_table, axis=1)
    where_slot = jnp.where(found_any, jnp.argmax(match_table, axis=1).astype(jnp.int32), SLOTS)
    where_slot = jnp.concatenate([where_slot, jnp.full((1,), SLOTS, jnp.int32)])
    near_ids = neighbors[slot_tile]
    near_slot = where_slot[near_ids]
    return slot_tile, live_slots, near_slot


def append_zero(table):
    return jnp.concatenate([table, jnp.zeros((1,) + table.shape[1:], table.dtype)], axis=0)


def stride_conv(feature_grid, near_slot, kernel, live_scale):
    side_len = feature_grid.shape[1]
    last_rows = append_zero(feature_grid[:, side_len - 1])
    last_cols = append_zero(feature_grid[:, :, side_len - 1])
    upper = last_rows[near_slot[:, 0]]
    left_cols = last_cols[near_slot[:, 1]]
    corner = last_rows[near_slot[:, 2]][:, side_len - 1]
    top_row = jnp.concatenate([corner[:, None], upper], axis=1)
    widened = jnp.concatenate([left_cols[:, :, None], feature_grid], axis=2)
    padded = jnp.concatenate([top_row[:, None], widened], axis=1)
    summed = None
    for row_tap in range(3):
        for col_tap in range(3):
            tap_view = padded[:, row_tap:row_tap + side_len - 1:2, col_tap:col_tap + side_len - 1:2]
            tap_term = jnp.einsum('srwc,co->srwo', tap_view.astype(jnp.float32), kernel[row_tap, col_tap].astype(jnp.float32))
            summed = tap_term if summed is None else summed + tap_term
    return (jax.nn.silu(summed) * live_scale[:, None, None, None]).astype(jnp.bfloat16)


def reference(state_tiles, water_mask, owner_tiles, neighbors, first_kernel, second_kernel, mix_kernel):
    slot_tile, live_slots, near_slot = slot_tables(water_mask, owner_tiles, neighbors)
    live_scale = live_slots.astype(jnp.float32)
    start_maps = jnp.transpose(state_tiles[slot_tile], (0, 2, 3, 1)) * live_slots.astype(jnp.bfloat16)[:, None, None, None]
    first_maps = stride_conv(start_maps, near_slot, first_kernel, live_scale)
    second_maps = stride_conv(first_maps, near_slot, second_kernel, live_scale)
    wide_maps = second_maps.astype(jnp.float32)
    pre_act = jnp.einsum('srwc,co->srwo', wide_maps, mix_kernel.astype(jnp.float32))
    return (wide_maps + jax.nn.silu(pre_act)).astype(jnp.bfloat16)
```

```python
import functools

import jax
import jax.numpy as jnp
import numpy as np
from jax import lax
from jax.experimental import pallas as pl
from jax.experimental.pallas import tpu as pltpu
from jax.sharding import PartitionSpec as P

BF16 = jnp.bfloat16
F32 = jnp.float32
REACH = 3
WINDOW = 8


def exact(spec, one_hot, values):
    return jnp.einsum(spec, one_hot, values, preferred_element_type=F32).astype(BF16)


def column_picker(width, slots):
    lanes = 128
    used = (lanes // (REACH * slots)) * REACH * slots
    count = width // 4
    picks = np.zeros((3, 3, count, lanes + width), np.float32)
    for tap in range(3):
        for kind in range(3):
            for at in range(count):
                col = 4 * at - 3 + 2 * kind + tap
                if col >= 0:
                    picks[tap, kind, at, lanes + col] = 1
                else:
                    picks[tap, kind, at, np.arange(col + REACH, used, REACH)] = 1
    return picks.reshape(9 * count, lanes + width)


def silu(x):
    return x * (1.0 / (1.0 + jnp.exp(-x)))


def tile_kernel(
    slots,
    table,
    slab_ref,
    halo_ref,
    picks_ref,
    first_ref,
    second_ref,
    mix_ref,
    out_ref,
    raw,
    maps,
):
    k = pl.program_id(0)
    rows, chans, width = slab_ref.shape[1:]
    blocks = rows // 4
    count = width // 4
    per = 128 // (REACH * slots)
    own_live = table[2, k].astype(F32)
    row_live = table[3, k].astype(F32)
    col_live = table[4, k].astype(F32)
    corner_live = table[5, k].astype(F32)

    pad = jnp.zeros((2, chans, 128 + width), BF16)
    raw[0:2] = pad
    raw[rows + 5 : rows + 7] = pad
    raw[rows + 6 : rows + 8] = pad
    raw[2:5, :, 128:] = halo_ref[pl.ds(REACH * k, REACH)]
    raw[5 : 5 + rows, :, 128:] = slab_ref[0]
    lane = lax.broadcasted_iota(jnp.int32, (chans, 128), 1)
    for at in range(rows + REACH):
        low = (at % per) * REACH * slots + REACH * k
        inside = (lane >= low) & (lane < low + REACH)
        tile = halo_ref[REACH * slots + at // per].astype(F32)
        raw[2 + at, :, :128] = jnp.where(inside, tile, 0.0).astype(BF16)

    across = (((1,), (1,)), ((), ()))
    whole = (rows // WINDOW + 1) * WINDOW
    even = lax.dot_general(
        picks_ref[...],
        raw[0:whole].reshape(whole * chans, 128 + width),
        across,
        preferred_element_type=F32,
    ).astype(BF16)
    odd = lax.dot_general(
        picks_ref[...],
        raw[4 : 4 + rows].reshape(rows * chans, 128 + width),
        across,
        preferred_element_type=F32,
    ).astype(BF16)
    span = WINDOW * chans
    kinds = 3 * count
    row_at = lax.broadcasted_iota(jnp.int32, (kinds, 1), 0)
    for n in range(blocks + 1):
        source = even if n % 2 == 0 else odd
        lo = (n // 2) * span
        patch = jnp.concatenate(
            [source[b * kinds : (b + 1) * kinds, lo : lo + span] for b in range(3)], axis=1
        )
        got = silu(jnp.dot(patch, first_ref[...], preferred_element_type=F32))
        if n == 0:
            keep = jnp.where(row_at == 0, corner_live, row_live)
        else:
            keep = jnp.where(row_at == 0, col_live, 1.0)
        maps[n] = (got * keep).astype(BF16)

    mid = second_ref.shape[1] // 3
    total = None
    for b in range(3):
        upper = maps[0:blocks, b * count : (b + 1) * count, mid:].reshape(blocks * count, mid)
        lower = maps[1 : blocks + 1, b * count : (b + 1) * count, :].reshape(
            blocks * count, 2 * mid
        )
        term = jnp.dot(upper, second_ref[b, :mid], preferred_element_type=F32)
        term += jnp.dot(lower, second_ref[b, mid:], preferred_element_type=F32)
        total = term if total is None else total + term
    second = (silu(total) * own_live).astype(BF16)
    pre_act = jnp.dot(second, mix_ref[...], preferred_element_type=F32)
    out = (second.astype(F32) + silu(pre_act)).astype(BF16)
    out_ref[0] = out.reshape(blocks, count, out.shape[-1])


def body(state_tiles, water_mask, owner_tiles, neighbors, first_kernel, second_kernel, mix_kernel):
    owners = lax.axis_size("space")
    owner_index = lax.axis_index("space")
    groups = lax.axis_size(("chan", "sub"))
    group = lax.axis_index(("chan", "sub"))
    held, chans, rows, width = state_tiles.shape
    slots = owner_tiles.shape[1]
    tiles = water_mask.shape[0]
    lanes = (held + owners - 1) // owners
    per = 128 // (REACH * slots)
    col_tiles = (rows + REACH + per - 1) // per

    last_rows = lax.ppermute(
        state_tiles[:, :, rows - REACH :, :],
        ("chan", "sub"),
        [(i, (i + 1) % groups) for i in range(groups)],
    )

    tile_ids = jnp.arange(tiles, dtype=jnp.int32)
    local_ids = owner_index * held + jnp.arange(held, dtype=jnp.int32)
    local_water = lax.dynamic_slice_in_dim(water_mask, owner_index * held, held)
    wanted = jnp.concatenate([neighbors, tile_ids[:, None]], axis=1)
    held_as = ((wanted[:, :, None] == local_ids) & (local_water > 0)).astype(BF16)
    stands = (owner_tiles.reshape(-1)[:, None] == tile_ids[None, :]).astype(BF16)
    sel = exact("pt,tdj->pdj", stands, held_as).reshape(owners, slots, 4, held)
    first_group = group == 0
    sel_row = jnp.where(first_group, sel[:, :, 0], sel[:, :, 3])
    sel_col = sel[:, :, 1]
    sel_corner = jnp.where(first_group, sel[:, :, 2], sel[:, :, 1])
    from_here = jnp.sum(sel[:, :, 3].astype(F32), axis=2)
    order = jnp.cumsum(from_here, axis=1) - 1
    lane_ids = jnp.arange(lanes, dtype=F32)
    in_lane = (order[:, :, None] == lane_ids).astype(BF16)
    choose = exact("okq,okj->oqj", in_lane, sel[:, :, 3])

    slabs = exact("oqj,jcrw->oqrcw", choose, state_tiles).reshape(
        owners, lanes * rows, chans, width
    )
    row_part = exact("okj,jcyw->okycw", sel_row, last_rows).reshape(
        owners, slots * REACH, chans, width
    )
    col_own = exact("okj,jcyb->oyckb", sel_col, state_tiles[:, :, :, width - REACH :])
    col_corner = exact("okj,jcyb->oyckb", sel_corner, last_rows[:, :, :, width - REACH :])
    cols = jnp.concatenate([col_corner, col_own], axis=1)
    cols = jnp.pad(
        cols.reshape(owners, rows + REACH, chans, slots * REACH),
        ((0, 0), (0, col_tiles * per - rows - REACH), (0, 0), (0, 0)),
    )
    cols = cols.reshape(owners, col_tiles, per, chans, slots * REACH)
    cols = jnp.transpose(cols, (0, 1, 3, 2, 4)).reshape(
        owners, col_tiles, chans, per * slots * REACH
    )
    cols = jnp.pad(cols, ((0, 0), (0, 0), (0, 0), (0, width - per * slots * REACH)))
    outgoing = jnp.concatenate([slabs, row_part, cols], axis=1)
    incoming = lax.all_to_all(outgoing, "space", split_axis=0, concat_axis=0, tiled=True)
    halo = jnp.sum(incoming[:, lanes * rows :].astype(F32), axis=0).astype(BF16)

    my_tiles = lax.dynamic_slice_in_dim(owner_tiles, owner_index, 1, 0)[0]
    mine = my_tiles[:, None] == tile_ids[None, :]
    alive = jnp.sum(
        jnp.where(wanted[:, :, None] == tile_ids, water_mask, 0), axis=2
    )
    my_alive = jnp.sum(jnp.where(mine[:, :, None], alive[None], 0), axis=1)
    my_live = my_alive[:, 3]
    source = my_tiles // held
    ids = jnp.arange(slots, dtype=jnp.int32)
    earlier = (
        (source[:, None] == source[None, :]) & (my_live[None, :] > 0) & (ids[None, :] < ids[:, None])
    )
    lane_of = jnp.minimum(jnp.sum(earlier.astype(jnp.int32), axis=1), lanes - 1)
    table = jnp.stack(
        [
            source,
            lane_of,
            my_live,
            jnp.where(first_group, my_alive[:, 0], 1),
            my_alive[:, 1],
            jnp.where(first_group, my_alive[:, 2], my_alive[:, 1]),
        ]
    ).astype(jnp.int32)

    full_mix = lax.all_gather(mix_kernel, ("chan", "sub"), axis=1, tiled=True)
    mid, deep = second_kernel.shape[2:]
    by_col = jnp.transpose(first_kernel, (1, 0, 2, 3))
    spare = WINDOW - 3
    first_weights = jnp.stack(
        [
            jnp.pad(by_col, ((0, 0), (0, spare), (0, 0), (0, 0))),
            jnp.pad(by_col, ((0, 0), (2, spare - 2), (0, 0), (0, 0))),
        ],
        axis=3,
    ).reshape(3 * WINDOW * chans, 2 * mid)
    second_weights = jnp.transpose(second_kernel, (1, 0, 2, 3)).reshape(3, 3 * mid, deep)
    picks = jnp.asarray(column_picker(width, slots), BF16)

    blocks, count = rows // 4, width // 4
    fixed = lambda *dims: pl.BlockSpec(dims, lambda k, t: (0,) * len(dims))
    return pl.pallas_call(
        functools.partial(tile_kernel, slots),
        grid_spec=pltpu.PrefetchScalarGridSpec(
            num_scalar_prefetch=1,
            grid=(slots,),
            in_specs=[
                pl.BlockSpec((1, rows, chans, width), lambda k, t: (t[0, k], t[1, k], 0, 0)),
                fixed(*halo.shape),
                fixed(*picks.shape),
                fixed(*first_weights.shape),
                fixed(*second_weights.shape),
                fixed(*full_mix.shape),
            ],
            out_specs=pl.BlockSpec((1, blocks, count, deep), lambda k, t: (k, 0, 0, 0)),
            scratch_shapes=[
                pltpu.VMEM((rows + WINDOW, chans, 128 + width), BF16),
                pltpu.VMEM((blocks + 1, 3 * count, 2 * mid), BF16),
            ],
        ),
        out_shape=jax.ShapeDtypeStruct((slots, blocks, count, deep), BF16),
        compiler_params=pltpu.CompilerParams(vmem_limit_bytes=48 * 1024 * 1024),
        cost_estimate=pl.CostEstimate(
            flops=8 * 10**9, bytes_accessed=10 * 10**6, transcendentals=10 * 10**6
        ),
    )(table, incoming, halo, picks, first_weights, second_weights, full_mix)


def solution(mesh):
    placed = (
        P(("ens", "space"), None, ("chan", "sub"), None),
        P(),
        P(),
        P(),
        P(),
        P(),
        P(None, ("chan", "sub")),
    )
    return jax.shard_map(
        body,
        mesh=mesh,
        in_specs=placed,
        out_specs=P(("ens", "space"), ("chan", "sub"), None, None),
        check_vma=False,
    )
```

```python
import functools

import jax
import jax.numpy as jnp
import numpy as np
from jax import lax
from jax.experimental import pallas as pl
from jax.experimental.pallas import tpu as pltpu
from jax.sharding import PartitionSpec as P

BF16 = jnp.bfloat16
F32 = jnp.float32
REACH = 3
WINDOW = 8


def exact(spec, one_hot, values):
    return jnp.einsum(spec, one_hot, values, preferred_element_type=F32).astype(BF16)


def column_picker(width, slots):
    lanes = 128
    used = (lanes // (REACH * slots)) * REACH * slots
    count = width // 4
    picks = np.zeros((3, 3, count, lanes + width), np.float32)
    for tap in range(3):
        for kind in range(3):
            for at in range(count):
                col = 4 * at - 3 + 2 * kind + tap
                if col >= 0:
                    picks[tap, kind, at, lanes + col] = 1
                else:
                    picks[tap, kind, at, np.arange(col + REACH, used, REACH)] = 1
    return picks.reshape(9 * count, lanes + width)


def silu(x):
    return x * (1.0 / (1.0 + jnp.exp(-x)))


def tile_kernel(
    slots,
    base,
    table,
    slab_ref,
    extra_ref,
    halo_ref,
    picks_ref,
    first_ref,
    second_ref,
    mix_ref,
    out_ref,
    raw,
    maps,
):
    k = pl.program_id(0)
    rows, chans, width = slab_ref.shape[1:]
    blocks = rows // 4
    count = width // 4
    per = 128 // (REACH * slots)
    own_live = table[2, k].astype(F32)
    row_live = table[3, k].astype(F32)
    col_live = table[4, k].astype(F32)
    corner_live = table[5, k].astype(F32)

    pad = jnp.zeros((2, chans, 128 + width), BF16)
    raw[0:2] = pad
    raw[rows + 5 : rows + 7] = pad
    raw[rows + 6 : rows + 8] = pad
    raw[2:5, :, 128:] = halo_ref[pl.ds(REACH * k, REACH)]
    in_base = table[1, k] < base

    @pl.when(in_base)
    def _():
        raw[5 : 5 + rows, :, 128:] = slab_ref[0]

    @pl.when(jnp.logical_not(in_base))
    def _():
        raw[5 : 5 + rows, :, 128:] = extra_ref[0]

    lane = lax.broadcasted_iota(jnp.int32, (chans, 128), 1)
    for at in range(rows + REACH):
        low = (at % per) * REACH * slots + REACH * k
        inside = (lane >= low) & (lane < low + REACH)
        tile = halo_ref[REACH * slots + at // per].astype(F32)
        raw[2 + at, :, :128] = jnp.where(inside, tile, 0.0).astype(BF16)

    across = (((1,), (1,)), ((), ()))
    whole = (rows // WINDOW + 1) * WINDOW
    even = lax.dot_general(
        picks_ref[...],
        raw[0:whole].reshape(whole * chans, 128 + width),
        across,
        preferred_element_type=F32,
    ).astype(BF16)
    odd = lax.dot_general(
        picks_ref[...],
        raw[4 : 4 + rows].reshape(rows * chans, 128 + width),
        across,
        preferred_element_type=F32,
    ).astype(BF16)
    span = WINDOW * chans
    kinds = 3 * count
    row_at = lax.broadcasted_iota(jnp.int32, (kinds, 1), 0)
    for n in range(blocks + 1):
        source = even if n % 2 == 0 else odd
        lo = (n // 2) * span
        patch = jnp.concatenate(
            [source[b * kinds : (b + 1) * kinds, lo : lo + span] for b in range(3)], axis=1
        )
        got = silu(jnp.dot(patch, first_ref[...], preferred_element_type=F32))
        if n == 0:
            keep = jnp.where(row_at == 0, corner_live, row_live)
        else:
            keep = jnp.where(row_at == 0, col_live, 1.0)
        maps[n] = (got * keep).astype(BF16)

    mid = second_ref.shape[1] // 3
    total = None
    for b in range(3):
        upper = maps[0:blocks, b * count : (b + 1) * count, mid:].reshape(blocks * count, mid)
        lower = maps[1 : blocks + 1, b * count : (b + 1) * count, :].reshape(
            blocks * count, 2 * mid
        )
        term = jnp.dot(upper, second_ref[b, :mid], preferred_element_type=F32)
        term += jnp.dot(lower, second_ref[b, mid:], preferred_element_type=F32)
        total = term if total is None else total + term
    second = (silu(total) * own_live).astype(BF16)
    pre_act = jnp.dot(second, mix_ref[...], preferred_element_type=F32)
    out = (second.astype(F32) + silu(pre_act)).astype(BF16)
    out_ref[0] = out.reshape(blocks, count, out.shape[-1])


def body(state_tiles, water_mask, owner_tiles, neighbors, first_kernel, second_kernel, mix_kernel):
    owners = lax.axis_size("space")
    owner_index = lax.axis_index("space")
    groups = lax.axis_size(("chan", "sub"))
    group = lax.axis_index(("chan", "sub"))
    held, chans, rows, width = state_tiles.shape
    slots = owner_tiles.shape[1]
    tiles = water_mask.shape[0]
    lanes = (held + owners - 1) // owners
    per = 128 // (REACH * slots)
    col_tiles = (rows + REACH + per - 1) // per

    tile_ids = jnp.arange(tiles, dtype=jnp.int32)
    local_ids = owner_index * held + jnp.arange(held, dtype=jnp.int32)
    local_water = lax.dynamic_slice_in_dim(water_mask, owner_index * held, held)
    wanted = jnp.concatenate([neighbors, tile_ids[:, None]], axis=1)
    held_as = ((wanted[:, :, None] == local_ids) & (local_water > 0)).astype(BF16)
    stands = (owner_tiles.reshape(-1)[:, None] == tile_ids[None, :]).astype(BF16)
    sel = exact("pt,tdj->pdj", stands, held_as).reshape(owners, slots, 4, held)
    first_group = group == 0
    sel_row = jnp.where(first_group, sel[:, :, 0], sel[:, :, 3])
    sel_col = sel[:, :, 1]
    sel_corner = jnp.where(first_group, sel[:, :, 2], sel[:, :, 1])
    from_here = jnp.sum(sel[:, :, 3].astype(F32), axis=2)
    order = jnp.cumsum(from_here, axis=1) - 1
    lane_ids = jnp.arange(lanes, dtype=F32)
    in_lane = (order[:, :, None] == lane_ids).astype(BF16)
    choose = exact("okq,okj->oqj", in_lane, sel[:, :, 3])

    slabs = exact("oqj,jcrw->oqrcw", choose, state_tiles).reshape(
        owners, lanes * rows, chans, width
    )
    base = (lanes + 1) // 2
    my_tiles = lax.dynamic_slice_in_dim(owner_tiles, owner_index, 1, 0)[0]
    mine = my_tiles[:, None] == tile_ids[None, :]
    alive = jnp.sum(
        jnp.where(wanted[:, :, None] == tile_ids, water_mask, 0), axis=2
    )
    my_alive = jnp.sum(jnp.where(mine[:, :, None], alive[None], 0), axis=1)
    my_live = my_alive[:, 3]
    source = my_tiles // held
    ids = jnp.arange(slots, dtype=jnp.int32)
    earlier = (
        (source[:, None] == source[None, :]) & (my_live[None, :] > 0) & (ids[None, :] < ids[:, None])
    )
    lane_of = jnp.minimum(jnp.sum(earlier.astype(jnp.int32), axis=1), lanes - 1)
    table = jnp.stack(
        [
            source,
            lane_of,
            my_live,
            jnp.where(first_group, my_alive[:, 0], 1),
            my_alive[:, 1],
            jnp.where(first_group, my_alive[:, 2], my_alive[:, 1]),
        ]
    ).astype(jnp.int32)

    def halo_out():
        last_rows = lax.ppermute(
            state_tiles[:, :, rows - REACH :, :],
            ("chan", "sub"),
            [(i, (i + 1) % groups) for i in range(groups)],
        )
        row_part = exact("okj,jcyw->okycw", sel_row, last_rows).reshape(
            owners, slots * REACH, chans, width
        )
        col_own = exact("okj,jcyb->oyckb", sel_col, state_tiles[:, :, :, width - REACH :])
        col_corner = exact("okj,jcyb->oyckb", sel_corner, last_rows[:, :, :, width - REACH :])
        cols = jnp.concatenate([col_corner, col_own], axis=1)
        cols = jnp.pad(
            cols.reshape(owners, rows + REACH, chans, slots * REACH),
            ((0, 0), (0, col_tiles * per - rows - REACH), (0, 0), (0, 0)),
        )
        cols = cols.reshape(owners, col_tiles, per, chans, slots * REACH)
        cols = jnp.transpose(cols, (0, 1, 3, 2, 4)).reshape(
            owners, col_tiles, chans, per * slots * REACH
        )
        cols = jnp.pad(cols, ((0, 0), (0, 0), (0, 0), (0, width - per * slots * REACH)))
        return jnp.concatenate([row_part, cols], axis=1)

    def weights():
        full_mix = lax.all_gather(mix_kernel, ("chan", "sub"), axis=1, tiled=True)
        mid, deep = second_kernel.shape[2:]
        by_col = jnp.transpose(first_kernel, (1, 0, 2, 3))
        spare = WINDOW - 3
        first_weights = jnp.stack(
            [
                jnp.pad(by_col, ((0, 0), (0, spare), (0, 0), (0, 0))),
                jnp.pad(by_col, ((0, 0), (2, spare - 2), (0, 0), (0, 0))),
            ],
            axis=3,
        ).reshape(3 * WINDOW * chans, 2 * mid)
        second_weights = jnp.transpose(second_kernel, (1, 0, 2, 3)).reshape(3, 3 * mid, deep)
        picks = jnp.asarray(column_picker(width, slots), BF16)
        return picks, first_weights, second_weights, full_mix

    def exchange(heavy):
        def swap(x):
            return lax.all_to_all(x, "space", split_axis=0, concat_axis=0, tiled=True)

        def run(slabs):
            arrived = swap(slabs[:, : base * rows])
            rest = slabs[:, base * rows :]
            if base == lanes:
                extra = arrived
            elif heavy is None:
                extra = swap(rest)
            else:
                got = jnp.where(owner_index == heavy, rest[heavy], 0)
                for owner in range(owners):
                    if owner != heavy:
                        got += lax.ppermute(rest[owner], "space", [(heavy, owner)])
                extra = jnp.pad(
                    got[None], ((heavy, owners - 1 - heavy), (0, 0), (0, 0), (0, 0))
                )
            halo = jnp.sum(swap(halo_out()).astype(F32), axis=0).astype(BF16)
            return (arrived, extra, halo) + weights()

        return run

    if base == lanes:
        results = exchange(None)(slabs)
    else:
        live = jnp.sum(jnp.where(owner_tiles[:, :, None] == tile_ids, water_mask, 0), axis=2)
        source_of = owner_tiles // held
        counts = jnp.sum(
            (source_of[:, :, None] == jnp.arange(owners)) & (live[:, :, None] > 0), axis=1
        )
        is_heavy = jnp.max(counts, axis=0) > base
        only = jnp.sum(jnp.where(is_heavy, jnp.arange(owners), 0))
        branch = jnp.where(jnp.sum(is_heavy) == 1, only, owners)
        results = lax.switch(
            branch, [exchange(o) for o in range(owners)] + [exchange(None)], slabs
        )
    arrived, extra, halo, picks, first_weights, second_weights, full_mix = results
    mid, deep = second_kernel.shape[2:]

    blocks, count = rows // 4, width // 4
    fixed = lambda *dims: pl.BlockSpec(dims, lambda k, t: (0,) * len(dims))
    return pl.pallas_call(
        functools.partial(tile_kernel, slots, base),
        grid_spec=pltpu.PrefetchScalarGridSpec(
            num_scalar_prefetch=1,
            grid=(slots,),
            in_specs=[
                pl.BlockSpec(
                    (1, rows, chans, width),
                    lambda k, t: (t[0, k], jnp.minimum(t[1, k], base - 1), 0, 0),
                ),
                pl.BlockSpec(
                    (1, rows, chans, width),
                    lambda k, t: (t[0, k], jnp.maximum(t[1, k] - base, 0), 0, 0),
                ),
                fixed(*halo.shape),
                fixed(*picks.shape),
                fixed(*first_weights.shape),
                fixed(*second_weights.shape),
                fixed(*full_mix.shape),
            ],
            out_specs=pl.BlockSpec((1, blocks, count, deep), lambda k, t: (k, 0, 0, 0)),
            scratch_shapes=[
                pltpu.VMEM((rows + WINDOW, chans, 128 + width), BF16),
                pltpu.VMEM((blocks + 1, 3 * count, 2 * mid), BF16),
            ],
        ),
        out_shape=jax.ShapeDtypeStruct((slots, blocks, count, deep), BF16),
        compiler_params=pltpu.CompilerParams(vmem_limit_bytes=48 * 1024 * 1024),
        cost_estimate=pl.CostEstimate(
            flops=8 * 10**9, bytes_accessed=10 * 10**6, transcendentals=10 * 10**6
        ),
    )(table, arrived, extra, halo, picks, first_weights, second_weights, full_mix)


def solution(mesh):
    placed = (
        P(("ens", "space"), None, ("chan", "sub"), None),
        P(),
        P(),
        P(),
        P(),
        P(),
        P(None, ("chan", "sub")),
    )
    return jax.shard_map(
        body,
        mesh=mesh,
        in_specs=placed,
        out_specs=P(("ens", "space"), ("chan", "sub"), None, None),
        check_vma=False,
    )
```

```python
import functools

import jax
import jax.numpy as jnp
import numpy as np
from jax import lax
from jax.experimental import pallas as pl
from jax.experimental.pallas import tpu as pltpu
from jax.sharding import PartitionSpec as P

BF16 = jnp.bfloat16
F32 = jnp.float32
REACH = 3
WINDOW = 8


def exact(spec, one_hot, values):
    return jnp.einsum(spec, one_hot, values, preferred_element_type=F32).astype(BF16)


def column_picker(width, slots):
    lanes = 128
    used = (lanes // (REACH * slots)) * REACH * slots
    count = width // 4
    picks = np.zeros((3, 3, count, lanes + width), np.float32)
    for tap in range(3):
        for kind in range(3):
            for at in range(count):
                col = 4 * at - 3 + 2 * kind + tap
                if col >= 0:
                    picks[tap, kind, at, lanes + col] = 1
                else:
                    picks[tap, kind, at, np.arange(col + REACH, used, REACH)] = 1
    return picks.reshape(9 * count, lanes + width)


def silu(x):
    return x * (1.0 / (1.0 + jnp.exp(-x)))


def tile_kernel(slots, table, *refs):
    slab_refs = refs[:-8]
    halo_ref, picks_ref, first_ref, second_ref, mix_ref, out_ref, raw, maps = refs[-8:]
    k = pl.program_id(0)
    rows, chans, width = slab_refs[0].shape[1:]
    blocks = rows // 4
    count = width // 4
    per = 128 // (REACH * slots)
    own_live = table[2, k].astype(F32)
    row_live = table[3, k].astype(F32)
    col_live = table[4, k].astype(F32)
    corner_live = table[5, k].astype(F32)

    pad = jnp.zeros((2, chans, 128 + width), BF16)
    raw[0:2] = pad
    raw[rows + 5 : rows + 7] = pad
    raw[rows + 6 : rows + 8] = pad
    raw[2:5, :, 128:] = halo_ref[pl.ds(REACH * k, REACH)]
    for shift, slab_ref in enumerate(slab_refs):

        @pl.when(table[0, k] == shift)
        def _(slab_ref=slab_ref):
            raw[5 : 5 + rows, :, 128:] = slab_ref[0]

    lane = lax.broadcasted_iota(jnp.int32, (chans, 128), 1)
    for at in range(rows + REACH):
        low = (at % per) * REACH * slots + REACH * k
        inside = (lane >= low) & (lane < low + REACH)
        tile = halo_ref[REACH * slots + at // per].astype(F32)
        raw[2 + at, :, :128] = jnp.where(inside, tile, 0.0).astype(BF16)

    across = (((1,), (1,)), ((), ()))
    whole = (rows // WINDOW + 1) * WINDOW
    even = lax.dot_general(
        picks_ref[...],
        raw[0:whole].reshape(whole * chans, 128 + width),
        across,
        preferred_element_type=F32,
    ).astype(BF16)
    odd = lax.dot_general(
        picks_ref[...],
        raw[4 : 4 + rows].reshape(rows * chans, 128 + width),
        across,
        preferred_element_type=F32,
    ).astype(BF16)
    span = WINDOW * chans
    kinds = 3 * count
    row_at = lax.broadcasted_iota(jnp.int32, (kinds, 1), 0)
    for n in range(blocks + 1):
        source = even if n % 2 == 0 else odd
        lo = (n // 2) * span
        patch = jnp.concatenate(
            [source[b * kinds : (b + 1) * kinds, lo : lo + span] for b in range(3)], axis=1
        )
        got = silu(jnp.dot(patch, first_ref[...], preferred_element_type=F32))
        if n == 0:
            keep = jnp.where(row_at == 0, corner_live, row_live)
        else:
            keep = jnp.where(row_at == 0, col_live, 1.0)
        maps[n] = (got * keep).astype(BF16)

    mid = second_ref.shape[1] // 3
    total = None
    for b in range(3):
        upper = maps[0:blocks, b * count : (b + 1) * count, mid:].reshape(blocks * count, mid)
        lower = maps[1 : blocks + 1, b * count : (b + 1) * count, :].reshape(
            blocks * count, 2 * mid
        )
        term = jnp.dot(upper, second_ref[b, :mid], preferred_element_type=F32)
        term += jnp.dot(lower, second_ref[b, mid:], preferred_element_type=F32)
        total = term if total is None else total + term
    second = (silu(total) * own_live).astype(BF16)
    pre_act = jnp.dot(second, mix_ref[...], preferred_element_type=F32)
    out = (second.astype(F32) + silu(pre_act)).astype(BF16)
    out_ref[0] = out.reshape(blocks, count, out.shape[-1])


def body(state_tiles, water_mask, owner_tiles, neighbors, first_kernel, second_kernel, mix_kernel):
    owners = lax.axis_size("space")
    owner_index = lax.axis_index("space")
    groups = lax.axis_size(("chan", "sub"))
    group = lax.axis_index(("chan", "sub"))
    held, chans, rows, width = state_tiles.shape
    slots = owner_tiles.shape[1]
    tiles = water_mask.shape[0]
    lanes = (held + owners - 1) // owners
    per = 128 // (REACH * slots)
    col_tiles = (rows + REACH + per - 1) // per

    last_rows = lax.ppermute(
        state_tiles[:, :, rows - REACH :, :],
        ("chan", "sub"),
        [(i, (i + 1) % groups) for i in range(groups)],
    )

    tile_ids = jnp.arange(tiles, dtype=jnp.int32)
    local_ids = owner_index * held + jnp.arange(held, dtype=jnp.int32)
    local_water = lax.dynamic_slice_in_dim(water_mask, owner_index * held, held)
    wanted = jnp.concatenate([neighbors, tile_ids[:, None]], axis=1)
    held_as = ((wanted[:, :, None] == local_ids) & (local_water > 0)).astype(BF16)
    turned = lax.dynamic_slice_in_dim(
        jnp.concatenate([owner_tiles, owner_tiles], axis=0), owner_index, owners, 0
    )
    stands = (turned.reshape(-1)[:, None] == tile_ids[None, :]).astype(BF16)
    sel = exact("pt,tdj->pdj", stands, held_as).reshape(owners, slots, 4, held)
    first_group = group == 0
    sel_row = jnp.where(first_group, sel[:, :, 0], sel[:, :, 3])
    sel_col = sel[:, :, 1]
    sel_corner = jnp.where(first_group, sel[:, :, 2], sel[:, :, 1])
    from_here = jnp.sum(sel[:, :, 3].astype(F32), axis=2)
    order = jnp.cumsum(from_here, axis=1) - 1
    lane_ids = jnp.arange(lanes, dtype=F32)
    in_lane = (order[:, :, None] == lane_ids).astype(BF16)
    choose = exact("okq,okj->oqj", in_lane, sel[:, :, 3])

    def send(shift, x):
        if shift == 0:
            return x
        return lax.ppermute(x, "space", [(i, (i + shift) % owners) for i in range(owners)])

    slabs = [None] * owners
    for shift in list(range(1, owners)) + [0]:
        slab = exact("qj,jcrw->qrcw", choose[shift], state_tiles)
        slabs[shift] = send(shift, slab)

    row_part = exact("okj,jcyw->okycw", sel_row, last_rows).reshape(
        owners, slots * REACH, chans, width
    )
    col_own = exact("okj,jcyb->oyckb", sel_col, state_tiles[:, :, :, width - REACH :])
    col_corner = exact("okj,jcyb->oyckb", sel_corner, last_rows[:, :, :, width - REACH :])
    cols = jnp.concatenate([col_corner, col_own], axis=1)
    cols = jnp.pad(
        cols.reshape(owners, rows + REACH, chans, slots * REACH),
        ((0, 0), (0, col_tiles * per - rows - REACH), (0, 0), (0, 0)),
    )
    cols = cols.reshape(owners, col_tiles, per, chans, slots * REACH)
    cols = jnp.transpose(cols, (0, 1, 3, 2, 4)).reshape(
        owners, col_tiles, chans, per * slots * REACH
    )
    cols = jnp.pad(cols, ((0, 0), (0, 0), (0, 0), (0, width - per * slots * REACH)))
    outgoing = jnp.concatenate([row_part, cols], axis=1)
    halo = sum(send(shift, outgoing[shift]).astype(F32) for shift in range(owners)).astype(BF16)

    my_tiles = turned[0]
    mine = my_tiles[:, None] == tile_ids[None, :]
    alive = jnp.sum(
        jnp.where(wanted[:, :, None] == tile_ids, water_mask, 0), axis=2
    )
    my_alive = jnp.sum(jnp.where(mine[:, :, None], alive[None], 0), axis=1)
    my_live = my_alive[:, 3]
    source = my_tiles // held
    ids = jnp.arange(slots, dtype=jnp.int32)
    earlier = (
        (source[:, None] == source[None, :]) & (my_live[None, :] > 0) & (ids[None, :] < ids[:, None])
    )
    lane_of = jnp.minimum(jnp.sum(earlier.astype(jnp.int32), axis=1), lanes - 1)
    table = jnp.stack(
        [
            (owner_index - source + owners) % owners,
            lane_of,
            my_live,
            jnp.where(first_group, my_alive[:, 0], 1),
            my_alive[:, 1],
            jnp.where(first_group, my_alive[:, 2], my_alive[:, 1]),
        ]
    ).astype(jnp.int32)

    full_mix = lax.all_gather(mix_kernel, ("chan", "sub"), axis=1, tiled=True)
    mid, deep = second_kernel.shape[2:]
    by_col = jnp.transpose(first_kernel, (1, 0, 2, 3))
    spare = WINDOW - 3
    first_weights = jnp.stack(
        [
            jnp.pad(by_col, ((0, 0), (0, spare), (0, 0), (0, 0))),
            jnp.pad(by_col, ((0, 0), (2, spare - 2), (0, 0), (0, 0))),
        ],
        axis=3,
    ).reshape(3 * WINDOW * chans, 2 * mid)
    second_weights = jnp.transpose(second_kernel, (1, 0, 2, 3)).reshape(3, 3 * mid, deep)
    picks = jnp.asarray(column_picker(width, slots), BF16)

    blocks, count = rows // 4, width // 4
    fixed = lambda *dims: pl.BlockSpec(dims, lambda k, t: (0,) * len(dims))
    return pl.pallas_call(
        functools.partial(tile_kernel, slots),
        grid_spec=pltpu.PrefetchScalarGridSpec(
            num_scalar_prefetch=1,
            grid=(slots,),
            in_specs=[
                *[
                    pl.BlockSpec(
                        (1, rows, chans, width),
                        lambda k, t, d=d: (jnp.where(t[0, k] == d, t[1, k], 0), 0, 0, 0),
                    )
                    for d in range(owners)
                ],
                fixed(*halo.shape),
                fixed(*picks.shape),
                fixed(*first_weights.shape),
                fixed(*second_weights.shape),
                fixed(*full_mix.shape),
            ],
            out_specs=pl.BlockSpec((1, blocks, count, deep), lambda k, t: (k, 0, 0, 0)),
            scratch_shapes=[
                pltpu.VMEM((rows + WINDOW, chans, 128 + width), BF16),
                pltpu.VMEM((blocks + 1, 3 * count, 2 * mid), BF16),
            ],
        ),
        out_shape=jax.ShapeDtypeStruct((slots, blocks, count, deep), BF16),
        compiler_params=pltpu.CompilerParams(vmem_limit_bytes=48 * 1024 * 1024),
        cost_estimate=pl.CostEstimate(
            flops=8 * 10**9, bytes_accessed=10 * 10**6, transcendentals=10 * 10**6
        ),
    )(table, *slabs, halo, picks, first_weights, second_weights, full_mix)


def solution(mesh):
    placed = (
        P(("ens", "space"), None, ("chan", "sub"), None),
        P(),
        P(),
        P(),
        P(),
        P(),
        P(None, ("chan", "sub")),
    )
    return jax.shard_map(
        body,
        mesh=mesh,
        in_specs=placed,
        out_specs=P(("ens", "space"), ("chan", "sub"), None, None),
        check_vma=False,
    )
```

```python
import functools

import jax
import jax.numpy as jnp
import numpy as np
from jax import lax
from jax.experimental import pallas as pl
from jax.experimental.pallas import tpu as pltpu
from jax.sharding import PartitionSpec as P

BF16 = jnp.bfloat16
F32 = jnp.float32
REACH = 3
WINDOW = 8


def exact(spec, one_hot, values):
    return jnp.einsum(spec, one_hot, values, preferred_element_type=F32).astype(BF16)


def column_picker(width, slots):
    lanes = 128
    used = (lanes // (REACH * slots)) * REACH * slots
    count = width // 4
    picks = np.zeros((3, 3, count, lanes + width), np.float32)
    for tap in range(3):
        for kind in range(3):
            for at in range(count):
                col = 4 * at - 3 + 2 * kind + tap
                if col >= 0:
                    picks[tap, kind, at, lanes + col] = 1
                else:
                    picks[tap, kind, at, np.arange(col + REACH, used, REACH)] = 1
    return picks.reshape(9 * count, lanes + width)


def silu(x):
    return x * (1.0 / (1.0 + jnp.exp(-x)))


def tile_kernel(slots, table, *refs):
    slab_refs = refs[:-8]
    halo_ref, picks_ref, first_ref, second_ref, mix_ref, out_ref, raw, maps = refs[-8:]
    k = pl.program_id(0)
    rows, chans, width = slab_refs[0].shape[1:]
    blocks = rows // 4
    count = width // 4
    per = 128 // (REACH * slots)
    own_live = table[2, k].astype(F32)
    row_live = table[3, k].astype(F32)
    col_live = table[4, k].astype(F32)
    corner_live = table[5, k].astype(F32)

    pad = jnp.zeros((2, chans, 128 + width), BF16)
    raw[0:2] = pad
    raw[rows + 5 : rows + 7] = pad
    raw[rows + 6 : rows + 8] = pad
    raw[2:5, :, 128:] = halo_ref[pl.ds(REACH * k, REACH)]
    for shift, slab_ref in enumerate(slab_refs):

        @pl.when(table[0, k] == shift)
        def _(slab_ref=slab_ref):
            raw[5 : 5 + rows, :, 128:] = slab_ref[0]

    lane = lax.broadcasted_iota(jnp.int32, (chans, 128), 1)
    for at in range(rows + REACH):
        low = (at % per) * REACH * slots + REACH * k
        inside = (lane >= low) & (lane < low + REACH)
        tile = halo_ref[REACH * slots + at // per].astype(F32)
        raw[2 + at, :, :128] = jnp.where(inside, tile, 0.0).astype(BF16)

    across = (((1,), (1,)), ((), ()))
    whole = (rows // WINDOW + 1) * WINDOW
    even = lax.dot_general(
        picks_ref[...],
        raw[0:whole].reshape(whole * chans, 128 + width),
        across,
        preferred_element_type=F32,
    ).astype(BF16)
    odd = lax.dot_general(
        picks_ref[...],
        raw[4 : 4 + rows].reshape(rows * chans, 128 + width),
        across,
        preferred_element_type=F32,
    ).astype(BF16)
    span = WINDOW * chans
    kinds = 3 * count
    row_at = lax.broadcasted_iota(jnp.int32, (kinds, 1), 0)
    for n in range(blocks + 1):
        source = even if n % 2 == 0 else odd
        lo = (n // 2) * span
        patch = jnp.concatenate(
            [source[b * kinds : (b + 1) * kinds, lo : lo + span] for b in range(3)], axis=1
        )
        got = silu(jnp.dot(patch, first_ref[...], preferred_element_type=F32))
        if n == 0:
            keep = jnp.where(row_at == 0, corner_live, row_live)
        else:
            keep = jnp.where(row_at == 0, col_live, 1.0)
        maps[n] = (got * keep).astype(BF16)

    mid = second_ref.shape[1] // 3
    total = None
    for b in range(3):
        upper = maps[0:blocks, b * count : (b + 1) * count, mid:].reshape(blocks * count, mid)
        lower = maps[1 : blocks + 1, b * count : (b + 1) * count, :].reshape(
            blocks * count, 2 * mid
        )
        term = jnp.dot(upper, second_ref[b, :mid], preferred_element_type=F32)
        term += jnp.dot(lower, second_ref[b, mid:], preferred_element_type=F32)
        total = term if total is None else total + term
    second = (silu(total) * own_live).astype(BF16)
    pre_act = jnp.dot(second, mix_ref[...], preferred_element_type=F32)
    out = (second.astype(F32) + silu(pre_act)).astype(BF16)
    out_ref[0] = out.reshape(blocks, count, out.shape[-1])


def body(state_tiles, water_mask, owner_tiles, neighbors, first_kernel, second_kernel, mix_kernel):
    owners = lax.axis_size("space")
    owner_index = lax.axis_index("space")
    groups = lax.axis_size(("chan", "sub"))
    group = lax.axis_index(("chan", "sub"))
    held, chans, rows, width = state_tiles.shape
    slots = owner_tiles.shape[1]
    tiles = water_mask.shape[0]
    lanes = (held + owners - 1) // owners
    per = 128 // (REACH * slots)
    col_tiles = (rows + REACH + per - 1) // per

    last_rows = lax.ppermute(
        state_tiles[:, :, rows - REACH :, :],
        ("chan", "sub"),
        [(i, (i + 1) % groups) for i in range(groups)],
    )

    tile_ids = jnp.arange(tiles, dtype=jnp.int32)
    local_ids = owner_index * held + jnp.arange(held, dtype=jnp.int32)
    local_water = lax.dynamic_slice_in_dim(water_mask, owner_index * held, held)
    wanted = jnp.concatenate([neighbors, tile_ids[:, None]], axis=1)
    held_as = ((wanted[:, :, None] == local_ids) & (local_water > 0)).astype(BF16)
    turned = lax.dynamic_slice_in_dim(
        jnp.concatenate([owner_tiles, owner_tiles], axis=0), owner_index, owners, 0
    )
    stands = (turned.reshape(-1)[:, None] == tile_ids[None, :]).astype(BF16)
    sel = exact("pt,tdj->pdj", stands, held_as).reshape(owners, slots, 4, held)
    first_group = group == 0
    sel_row = jnp.where(first_group, sel[:, :, 0], sel[:, :, 3])
    sel_col = sel[:, :, 1]
    sel_corner = jnp.where(first_group, sel[:, :, 2], sel[:, :, 1])
    from_here = jnp.sum(sel[:, :, 3].astype(F32), axis=2)
    order = jnp.cumsum(from_here, axis=1) - 1
    lane_ids = jnp.arange(lanes, dtype=F32)
    in_lane = (order[:, :, None] == lane_ids).astype(BF16)
    choose = exact("okq,okj->oqj", in_lane, sel[:, :, 3])

    def send(shift, x):
        if shift == 0:
            return x
        return lax.ppermute(x, "space", [(i, (i + shift) % owners) for i in range(owners)])

    slabs = [None] * owners
    for shift in list(range(1, owners)) + [0]:
        slab = exact("qj,jcrw->qrcw", choose[shift], state_tiles)
        slabs[shift] = send(shift, slab)

    row_part = exact("okj,jcyw->okycw", sel_row, last_rows).reshape(
        owners, slots * REACH, chans, width
    )
    col_own = exact("okj,jcyb->oyckb", sel_col, state_tiles[:, :, :, width - REACH :])
    col_corner = exact("okj,jcyb->oyckb", sel_corner, last_rows[:, :, :, width - REACH :])
    cols = jnp.concatenate([col_corner, col_own], axis=1)
    cols = jnp.pad(
        cols.reshape(owners, rows + REACH, chans, slots * REACH),
        ((0, 0), (0, col_tiles * per - rows - REACH), (0, 0), (0, 0)),
    )
    cols = cols.reshape(owners, col_tiles, per, chans, slots * REACH)
    cols = jnp.transpose(cols, (0, 1, 3, 2, 4)).reshape(
        owners, col_tiles, chans, per * slots * REACH
    )
    cols = jnp.pad(cols, ((0, 0), (0, 0), (0, 0), (0, width - per * slots * REACH)))
    full_mix = lax.all_gather(mix_kernel, ("chan", "sub"), axis=1, tiled=True)
    outgoing = jnp.concatenate([row_part, cols], axis=1)
    outgoing, full_mix = lax.optimization_barrier((outgoing, full_mix))
    halo = sum(send(shift, outgoing[shift]).astype(F32) for shift in range(owners)).astype(BF16)

    my_tiles = turned[0]
    mine = my_tiles[:, None] == tile_ids[None, :]
    alive = jnp.sum(
        jnp.where(wanted[:, :, None] == tile_ids, water_mask, 0), axis=2
    )
    my_alive = jnp.sum(jnp.where(mine[:, :, None], alive[None], 0), axis=1)
    my_live = my_alive[:, 3]
    source = my_tiles // held
    ids = jnp.arange(slots, dtype=jnp.int32)
    earlier = (
        (source[:, None] == source[None, :]) & (my_live[None, :] > 0) & (ids[None, :] < ids[:, None])
    )
    lane_of = jnp.minimum(jnp.sum(earlier.astype(jnp.int32), axis=1), lanes - 1)
    table = jnp.stack(
        [
            (owner_index - source + owners) % owners,
            lane_of,
            my_live,
            jnp.where(first_group, my_alive[:, 0], 1),
            my_alive[:, 1],
            jnp.where(first_group, my_alive[:, 2], my_alive[:, 1]),
        ]
    ).astype(jnp.int32)

    mid, deep = second_kernel.shape[2:]
    by_col = jnp.transpose(first_kernel, (1, 0, 2, 3))
    spare = WINDOW - 3
    first_weights = jnp.stack(
        [
            jnp.pad(by_col, ((0, 0), (0, spare), (0, 0), (0, 0))),
            jnp.pad(by_col, ((0, 0), (2, spare - 2), (0, 0), (0, 0))),
        ],
        axis=3,
    ).reshape(3 * WINDOW * chans, 2 * mid)
    second_weights = jnp.transpose(second_kernel, (1, 0, 2, 3)).reshape(3, 3 * mid, deep)
    picks = jnp.asarray(column_picker(width, slots), BF16)

    blocks, count = rows // 4, width // 4
    fixed = lambda *dims: pl.BlockSpec(dims, lambda k, t: (0,) * len(dims))
    return pl.pallas_call(
        functools.partial(tile_kernel, slots),
        grid_spec=pltpu.PrefetchScalarGridSpec(
            num_scalar_prefetch=1,
            grid=(slots,),
            in_specs=[
                *[
                    pl.BlockSpec(
                        (1, rows, chans, width),
                        lambda k, t, d=d: (jnp.where(t[0, k] == d, t[1, k], 0), 0, 0, 0),
                    )
                    for d in range(owners)
                ],
                fixed(*halo.shape),
                fixed(*picks.shape),
                fixed(*first_weights.shape),
                fixed(*second_weights.shape),
                fixed(*full_mix.shape),
            ],
            out_specs=pl.BlockSpec((1, blocks, count, deep), lambda k, t: (k, 0, 0, 0)),
            scratch_shapes=[
                pltpu.VMEM((rows + WINDOW, chans, 128 + width), BF16),
                pltpu.VMEM((blocks + 1, 3 * count, 2 * mid), BF16),
            ],
        ),
        out_shape=jax.ShapeDtypeStruct((slots, blocks, count, deep), BF16),
        compiler_params=pltpu.CompilerParams(vmem_limit_bytes=48 * 1024 * 1024),
        cost_estimate=pl.CostEstimate(
            flops=8 * 10**9, bytes_accessed=10 * 10**6, transcendentals=10 * 10**6
        ),
    )(table, *slabs, halo, picks, first_weights, second_weights, full_mix)


def solution(mesh):
    placed = (
        P(("ens", "space"), None, ("chan", "sub"), None),
        P(),
        P(),
        P(),
        P(),
        P(),
        P(None, ("chan", "sub")),
    )
    return jax.shard_map(
        body,
        mesh=mesh,
        in_specs=placed,
        out_specs=P(("ens", "space"), ("chan", "sub"), None, None),
        check_vma=False,
    )
```
